32 devices in a mesh: row: 2 (over x), col: 4 (over y, core), vir: 4 (over z).
Axes of the slice: x: 2, y: 2, z: 4, core: 2. Of those that a mesh axis runs over, the one named last changes fastest.
Arguments:
- amplitudes: bfloat16 [64, 2, 16, 4, 2, 3, 1792], P(None, 'row', None, 'col'), may hold values from -6 to 6
- integrals: bfloat16 [64, 64, 3, 1792], P('vir', 'row', None, 'col'), may hold values from -0.25 to 0.25
- hole_integrals: bfloat16 [128, 16, 4, 2, 3, 64], P(None, None, 'col'), may hold values from -0.3125 to 0.3125
- irreps: int32 [112], replicated, may hold values from 0 to 7
- occ_energy: float32 [128], replicated, may hold values from -2 to -0.5
- vir_energy: float32 [64], replicated, may hold values from 0.5 to 3
Outputs:
- increment: bfloat16 [64, 2, 16, 4, 2, 64, 64], P(None, 'row', None, 'col', None, 'vir')
The draws below stay inside these ranges and needn't reach their ends.
All inputs are finite; a program needn't handle non-finite values.
Results may differ from the reference program's by a relative error of at most 0.001.
Values may be sent and summed in bfloat16 or wider, within the bound.
No kernel may reach another device: no remote copies, remote signals or barrier semaphores. Data moves between devices by JAX's collectives and lax.ppermute only.
A program may use at most 256 MiB of HBM per device.

```python
import jax
import jax.numpy as jnp
from jax import lax

NO = 128
NV = 1792
SA = 64
CW = 3
VBLK = 16
N_ROW = 2
N_COL = 4


def plant(drawn, key, least, largest):
    longest = drawn.shape.index(max(drawn.shape))
    spots = []
    for shift in (0, 1):
        where = [jax.random.randint(jax.random.fold_in(key, axis), (), 0, length) for axis, length in enumerate(drawn.shape)]
        where[longest] = (where[longest] + shift) % drawn.shape[longest]
        spots.append(tuple(where))
    return drawn.at[spots[0]].set(least).at[spots[1]].set(largest)


def level_of(stream_key, shape, shards, least, largest):
    gain, own = 1.0, jax.random.fold_in(stream_key, 6)
    for position, blocks in shards:
        steps = jnp.exp(jax.random.uniform(jax.random.fold_in(own, position), (blocks,), jnp.float32, least / len(shards), largest / len(shards)))
        gain = gain * jnp.repeat(steps, shape[position] // blocks).reshape([-1 if axis == position else 1 for axis in range(len(shape))])
    return gain


def noise(stream_key, extent, spread, bound, pieces=(), held_as=jnp.bfloat16):
    loudness = level_of(stream_key, extent, pieces, -0.22, 0.18) if pieces else 1.0
    values = jax.random.normal(stream_key, extent, jnp.float32) * spread * loudness
    return jnp.minimum(jnp.maximum(values, -bound), bound).astype(held_as)


def setup_inputs(seed: int = 0) -> dict:
    keys = jax.random.split(jax.random.key(seed), 7)
    amplitudes = noise(keys[0], (NO // N_ROW, N_ROW, NO // (N_ROW * N_COL), N_COL, N_ROW, CW, NV), 1.0, 6.0, ((1, 2), (3, 4)))
    integrals = noise(keys[1], (SA, SA, CW, NV), (CW * NV // 8) ** -0.5, 0.25, ((0, 4), (1, 2), (3, 4)))
    hole_integrals = noise(keys[2], (NO, NO // (N_ROW * N_COL), N_COL, N_ROW, CW, SA), (NO * CW) ** -0.5, 0.3125, ((2, 4),))
    irreps = plant(jax.random.randint(keys[3], (NV // VBLK,), 0, 8), jax.random.fold_in(keys[3], 1), 0, 7).astype(jnp.int32)
    occ_energy = jnp.clip(jax.random.uniform(keys[4], (NO,), jnp.float32, -2.0, -0.5), -2.0, -0.5)
    vir_energy = jnp.clip(jax.random.uniform(keys[5], (SA,), jnp.float32, 0.5, 3.0), 0.5, 3.0)
    return dict(amplitudes=amplitudes, integrals=integrals, hole_integrals=hole_integrals, irreps=irreps, occ_energy=occ_energy, vir_energy=vir_energy)


def reference(amplitudes, integrals, hole_integrals, irreps, occ_energy, vir_energy):
    amps = amplitudes.reshape(NO, NO, CW, NV)
    wmat = hole_integrals.reshape(NO, NO, CW, SA).astype(jnp.float32)
    labels = jnp.repeat(irreps, VBLK)
    left = jnp.bitwise_xor(labels[:SA][:, None], labels[:SA][None, :])
    right = jnp.bitwise_xor(labels[:CW][:, None], labels[None, :])
    keep = left[:, :, None, None] == right[None, None, :, :]
    masked = jnp.where(keep, integrals, jnp.zeros_like(integrals)).astype(jnp.float32)
    slab_amps = amps[:, :, :, :SA]

    def per_row(index):
        first = lax.dynamic_index_in_dim(amps, index, 0, keepdims=False).astype(jnp.float32)
        ladder = lax.dot_general(first, masked, (((1, 2), (2, 3)), ((), ())), preferred_element_type=jnp.float32)
        along = lax.dynamic_index_in_dim(slab_amps, index, 0, keepdims=False).astype(jnp.float32)
        crossed = -lax.dot_general(along, wmat, (((0, 1), (0, 2)), ((), ())), preferred_element_type=jnp.float32)
        return ladder + jnp.transpose(crossed, (1, 0, 2))

    mixed = lax.map(per_row, jnp.arange(NO, dtype=jnp.int32))
    summed = mixed + jnp.transpose(mixed, (1, 0, 3, 2))
    denom = (occ_energy[:, None, None, None] + occ_energy[None, :, None, None]
             - vir_energy[None, None, :, None] - vir_energy[None, None, None, :])
    result = (summed / denom).astype(jnp.bfloat16)
    return result.reshape(NO // N_ROW, N_ROW, NO // (N_ROW * N_COL), N_COL, N_ROW, SA, SA)
```

```python
import functools

import jax
import jax.numpy as jnp
import numpy as np
from jax import lax
from jax.experimental import pallas as pl
from jax.experimental.pallas import tpu as pltpu
from jax.sharding import PartitionSpec as P

NO = 128
NV = 1792
SA = 64
CW = 3
VBLK = 16

LANES = 128
WIDE = VBLK * VBLK
ROOM = 10
AXES = ("row", "col", "vir")
BF = jnp.bfloat16
F32 = jnp.float32
GRAIN = 64.0
TOP = 32000.0
PARAMS = pltpu.CompilerParams(vmem_limit_bytes=56 * 1024 * 1024)
ANY = pl.BlockSpec(memory_space=pl.ANY)
PLACE = [b // 8 * 8 + b % 2 * 4 + b % 8 // 2 for b in range(VBLK)]
NAMED = [PLACE.index(p) for p in range(VBLK)]


def nt(left, right):
    return lax.dot_general(left, right, (((1,), (1,)), ((), ())), preferred_element_type=F32)


def cost(flops, moved):
    return pl.CostEstimate(flops=int(flops), bytes_accessed=int(moved), transcendentals=0)


def pack_kernel(spot_ref, irr_ref, turn_ref, v_ref, out_ref):
    depth = v_ref.shape[3]
    count = depth // VBLK
    lane = lax.broadcasted_iota(jnp.int32, (1, depth), 1)
    row = lax.broadcasted_iota(jnp.int32, (ROOM * VBLK, depth), 0)
    for half in range(2):
        label = irr_ref[spot_ref[2]] ^ irr_ref[2 * spot_ref[0] + half] ^ irr_ref[0]
        held = -spot_ref[3]
        target = jnp.full((1, depth), -1, jnp.int32)
        for block in range(count):
            match = irr_ref[spot_ref[1] * count + block] == label
            start = jnp.where(match & (held >= 0), held * VBLK, -NV)
            target = jnp.where(lane // VBLK == block, start + lane % VBLK, target)
            held = held + match.astype(jnp.int32)
        pick = (row == target).astype(F32).astype(BF)
        for c in range(CW):
            part = v_ref[:, c, half * VBLK : (half + 1) * VBLK, :].reshape(WIDE, depth)
            packed = nt(pick, part).astype(BF)
            out_ref[half, c] = jnp.dot(packed, turn_ref[...], preferred_element_type=F32).astype(BF)


def pack(spot, irreps, turn, v):
    return pl.pallas_call(
        pack_kernel,
        grid_spec=pltpu.PrefetchScalarGridSpec(
            num_scalar_prefetch=2,
            grid=(1,),
            in_specs=[
                pl.BlockSpec(turn.shape, lambda i, *_: (0, 0)),
                pl.BlockSpec(v.shape, lambda i, *_: (0, 0, 0, 0)),
            ],
            out_specs=pl.BlockSpec((2, CW, ROOM * VBLK, WIDE), lambda i, *_: (0, 0, 0, 0)),
        ),
        out_shape=jax.ShapeDtypeStruct((2, CW, ROOM * VBLK, WIDE), BF),
        compiler_params=PARAMS,
        cost_estimate=cost(4e8, 2e6),
    )(spot, irreps, turn, v)


def unpack_kernel(n_col, spot_ref, irr_ref, near_ref, far_ref, out_ref, found_ref):
    step = pl.program_id(0)
    other = spot_ref[2] ^ jnp.where(step == 0, 3, step - 1)
    label = irr_ref[spot_ref[2]] ^ irr_ref[other] ^ irr_ref[0]
    away = ((other // 2) != spot_ref[0]).astype(jnp.int32)
    base = jnp.where(step == 0, 8, away * 4 + other % 2)
    pace = jnp.where(step == 0, 1, 2)
    depth = NV // n_col
    count = depth // VBLK
    out_ref[...] = jnp.zeros(out_ref.shape, BF)
    for dc in range(n_col):
        shard = spot_ref[1] ^ dc
        piece_ref = far_ref if dc % 2 else near_ref
        which = base + (dc // 2) * pace

        def note(block, held):
            found_ref[jnp.clip(held + 1, 0, ROOM + 1)] = block
            return held + (irr_ref[shard * count + block] == label).astype(jnp.int32)

        held = lax.fori_loop(0, count, note, -spot_ref[3], unroll=count)

        def move(place, _):
            row = shard * depth + found_ref[place + 1] * VBLK
            for c in range(CW):
                out_ref[pl.ds(pl.multiple_of(c * NV + row, VBLK), VBLK), :] = piece_ref[
                    which, c, pl.ds(pl.multiple_of(place * VBLK, VBLK), VBLK), :
                ]
            return 0

        lax.fori_loop(0, jnp.clip(held, 0, ROOM), move, 0)


def unpack(spot, irreps, near, far, n_col):
    whole = pl.BlockSpec(near.shape, lambda t, *_: (0, 0, 0, 0))
    return pl.pallas_call(
        functools.partial(unpack_kernel, n_col),
        grid_spec=pltpu.PrefetchScalarGridSpec(
            num_scalar_prefetch=2,
            grid=(5,),
            in_specs=[whole, whole],
            out_specs=pl.BlockSpec((CW * NV, WIDE), lambda t, *_: (0, t)),
            scratch_shapes=[pltpu.SMEM((ROOM + 2,), jnp.int32)],
        ),
        out_shape=jax.ShapeDtypeStruct((CW * NV, 5 * WIDE), BF),
        compiler_params=PARAMS,
        cost_estimate=cost(1e6, 18e6),
    )(spot, irreps, near, far)


def chunk_kernel(spot_ref, t_ref, out_ref, slab_ref):
    groups, occ_h = t_ref.shape[0], t_ref.shape[2]
    rows = 2 * occ_h
    first = []
    for c in range(CW):
        part = t_ref[:, 0, :, c, :, :].reshape(groups * rows, NV)
        out_ref[0, :, c * NV : (c + 1) * NV] = part
        first.append(part[:, :LANES])
    row = lax.broadcasted_iota(jnp.int32, (2 * VBLK, LANES), 0)
    lane = lax.broadcasted_iota(jnp.int32, (2 * VBLK, LANES), 1)
    block = jnp.where(row < VBLK, spot_ref[2], spot_ref[2] ^ 3)
    pick = (lane == block * VBLK + row % VBLK).astype(F32).astype(BF)
    empty = jnp.zeros((rows, LANES), BF)
    for q in range(groups):
        some = jnp.concatenate([x[q * rows : (q + 1) * rows] for x in first] + [empty], axis=0)
        found = nt(pick, some).astype(BF)
        for far in range(2):
            slab_ref[far, 0, q * VBLK : (q + 1) * VBLK, :] = found[far * VBLK : (far + 1) * VBLK]


def chunk_amplitudes(spot, t, dcs):
    q4, n_col, occ_h, _, n_row, _ = t.shape
    some = 4
    rows = occ_h * n_row

    def group(i, spot):
        return spot[1] ^ jnp.where(i == 0, dcs[0], dcs[-1])

    return pl.pallas_call(
        chunk_kernel,
        grid_spec=pltpu.PrefetchScalarGridSpec(
            num_scalar_prefetch=1,
            grid=(len(dcs), q4 // some),
            in_specs=[
                pl.BlockSpec(
                    (some, 1, occ_h, CW, n_row, NV), lambda i, q, spot: (q, group(i, spot), 0, 0, 0, 0)
                )
            ],
            out_specs=[
                pl.BlockSpec((1, some * rows, CW * NV), lambda i, q, _: (i, q, 0)),
                pl.BlockSpec((2, 1, some * VBLK, LANES), lambda i, q, _: (0, i, q, 0)),
            ],
        ),
        out_shape=[
            jax.ShapeDtypeStruct((len(dcs), q4 * rows, CW * NV), BF),
            jax.ShapeDtypeStruct((2, len(dcs), q4 * VBLK, LANES), BF),
        ],
        compiler_params=PARAMS,
        cost_estimate=cost(1e8, 23e6),
    )(spot, t)


def trade_lanes(x, bits):
    piece = lax.broadcasted_iota(jnp.int32, x[0].shape, 1) // VBLK
    for k in range(bits):
        bit = 1 << k
        upper = (piece & bit) != 0
        y = []
        for i in range(1 << bits):
            if i & bit:
                moved = pltpu.roll(x[i ^ bit], LANES - bit * VBLK, 1)
                y.append(jnp.where(upper, x[i], moved))
            else:
                moved = pltpu.roll(x[i ^ bit], bit * VBLK, 1)
                y.append(jnp.where(upper, moved, x[i]))
        x = y
    return x


def mixed_kernel(n_col, spot_ref, t_ref, v_ref, w_ref, order_ref, *refs):
    parts, refs = refs[:n_col], refs[n_col:]
    u_ref, near0_ref, near1_ref, one_ref, two_ref, acc, zs, ints, slabs = refs
    step = pl.program_id(0)
    rows = 2 * WIDE

    def product():
        return jnp.dot(t_ref[0], v_ref[...], preferred_element_type=F32)

    def keep(ladder):
        for half in range(2):
            acc[half] = ladder[:, half * LANES : (half + 1) * LANES]

    def rest():
        holes = jnp.concatenate([w_ref[:, c].reshape(rows, NO) for c in range(CW)], axis=1)
        slab = slabs[(step == 1).astype(jnp.int32)]
        cross = jnp.dot(holes, slab, preferred_element_type=F32)
        for half in range(2):
            zs[half] = cross[:, half * LANES : (half + 1) * LANES]
        for lt in range(2):
            for s in range(2):
                for half in range(2):
                    for hh in range(2):
                        first = [
                            s * WIDE + NAMED[half * 8 + i] * VBLK + hh * 8 for i in range(8)
                        ]
                        x = trade_lanes([zs[lt, at : at + 8, :] for at in first], 3)
                        for j in range(8):
                            q4 = lt * 8 + j
                            have = acc[half, pl.ds(q4 * 32 + hh * 16 + s, 8, stride=2), :]
                            u_ref[
                                s, q4 * 16 + hh * 8 : q4 * 16 + hh * 8 + 8,
                                half * LANES : (half + 1) * LANES,
                            ] = have - x[j]
        for dr in range(2):
            value = u_ref[spot_ref[0] ^ dr]
            most = jnp.maximum(jnp.max(jnp.abs(value), axis=0, keepdims=True), 1e-30)
            grade = jnp.ceil(jnp.log2(most) * GRAIN)
            scale = TOP * jnp.exp2(-grade / GRAIN)
            whole = jnp.floor(value * scale + 0.5).astype(jnp.int32).astype(jnp.int16)
            grades = jnp.broadcast_to(grade, (16, WIDE)).astype(jnp.int32).astype(jnp.int16)
            ints[dr, :WIDE, :] = whole
            ints[dr, WIDE:, :] = grades

    @pl.when(step == 0)
    def _():
        order = jnp.concatenate([order_ref[spot_ref[1] ^ dc] for dc in range(n_col)], axis=1)
        for far in range(2):
            pieces = jnp.concatenate([part[0, far, 0] for part in parts], axis=1)
            slabs[far] = nt(order, pieces).astype(BF)
        keep(product())

    @pl.when((step > 0) & (step < 5))
    def _():
        ladder = product()
        rest()
        keep(ladder)

    @pl.when(step == 5)
    def _():
        rest()

    def send(outs):
        for dr in range(2):
            outs[dr][...] = ints[dr]

    for n, outs in (
        (1, (near0_ref.at[1], near1_ref.at[1])),
        (2, (near0_ref.at[0], near1_ref.at[0])),
        (3, (one_ref.at[0], one_ref.at[1])),
        (4, (two_ref.at[0], two_ref.at[1])),
    ):
        pl.when(step == n)(functools.partial(send, outs))


def mixed_group(dc, spot, t, at, v, w, order, near, far, n_col):
    ints = jax.ShapeDtypeStruct((2, WIDE + 16, WIDE), jnp.int16)
    ints_spec = pl.BlockSpec(ints.shape, lambda n, spot: (0, 0, 0))

    def slab_spec(other):
        group = dc ^ other
        which = (2 if group % 2 == 0 else 0) + other // 2
        return pl.BlockSpec(
            (1, 2, 1, WIDE, LANES), lambda n, spot: (which, 0, int(group < 2), 0, 0)
        )

    return pl.pallas_call(
        functools.partial(mixed_kernel, n_col),
        grid_spec=pltpu.PrefetchScalarGridSpec(
            num_scalar_prefetch=1,
            grid=(6,),
            in_specs=[
                pl.BlockSpec((1,) + t.shape[1:], lambda n, spot: (at, 0, 0)),
                pl.BlockSpec((CW * NV, WIDE), lambda n, spot: (0, jnp.minimum(n, 4))),
                pl.BlockSpec(
                    (2, CW, VBLK, w.shape[3], NO),
                    lambda n, spot: (0, 0, spot[2] ^ jnp.maximum(n - 2, 0), 0, 0),
                ),
                pl.BlockSpec(order.shape, lambda n, spot: (0, 0, 0)),
            ]
            + [slab_spec(other) for other in range(n_col)],
            out_specs=[
                pl.BlockSpec((2, WIDE, WIDE), lambda n, spot: (0, 0, jnp.clip(n - 2, 0, 3)))
            ]
            + [ints_spec] * 4,
            scratch_shapes=[
                pltpu.VMEM((2, 2 * WIDE, LANES), F32),
                pltpu.VMEM((2, 2 * WIDE, LANES), F32),
                pltpu.VMEM((2, WIDE + 16, WIDE), jnp.int16),
                pltpu.VMEM((2, CW * NO, WIDE), BF),
            ],
        ),
        out_shape=[jax.ShapeDtypeStruct((2, WIDE, 4 * WIDE), F32)] + [ints] * 4,
        compiler_params=PARAMS,
        cost_estimate=cost(7.2e9, 24e6),
    )(spot, t, v, w, order, *([near, far] * 2))


def trade_rows(x):
    row = lax.broadcasted_iota(jnp.int32, x[0].shape, 0)
    for k in range(3):
        bit = 1 << k
        upper = (row & bit) != 0
        y = []
        for i in range(8):
            if i & bit:
                y.append(jnp.where(upper, x[i], pltpu.roll(x[i ^ bit], 8 - bit, 0)))
            else:
                y.append(jnp.where(upper, pltpu.roll(x[i ^ bit], bit, 0), x[i]))
        x = y
    return x


def final_kernel(spot_ref, pair_ref, slab_ref, turn_ref, swap_ref, u_ref, *refs):
    got, (out_ref, ints, incs, os) = refs[:5], refs[-4:]
    step = pl.program_id(0)
    for dr in range(2):

        @pl.when(step == dr)
        def _(dr=dr):
            if dr == 0:
                near, one, two = got[0], got[1].at[0], got[2].at[0]
            else:
                near, one, two = got[3], got[4].at[0], got[4].at[1]
            ints[0], ints[1], ints[2], ints[3] = near[0], one[...], two[...], near[1]

    own = u_ref[0]
    high = own.astype(BF)
    low = (own - high.astype(F32)).astype(BF)
    both = jnp.concatenate([high, low], axis=1)
    both = jnp.dot(turn_ref[...], both, preferred_element_type=F32).astype(BF)
    both = jnp.concatenate([both[:, i * WIDE : (i + 1) * WIDE] for i in range(8)], axis=0)
    both = jnp.dot(both, swap_ref[...], preferred_element_type=F32)
    pair = pair_ref[0, 0]
    for t in range(4):
        mine = both[t * WIDE : (t + 1) * WIDE] + both[(t + 4) * WIDE : (t + 5) * WIDE]
        grade = ints[t, WIDE : WIDE + 16, :].astype(jnp.int32).astype(F32)[:1]
        scale = jnp.exp2(grade / GRAIN) / TOP
        mirror = ints[t, :WIDE, :].astype(jnp.int32).astype(F32) * scale
        incs[t] = (mine + mirror) / (pair - slab_ref[:, t * WIDE : (t + 1) * WIDE])
    for h in range(16):
        for q_half in range(2):
            rows = slice(h * 16 + q_half * 8, h * 16 + q_half * 8 + 8)
            x = []
            for half in range(2):
                lanes = slice(half * LANES, (half + 1) * LANES)
                x += trade_lanes([incs[spot_ref[2] ^ b, rows, lanes] for b in range(4)], 2)
            for p, pieces in enumerate(trade_rows(x)):
                first = ((q_half * 8 + p) * 16 + h) * VBLK
                os[pl.ds(first, 8, stride=2), :] = pieces
                os[pl.ds(first + 1, 8, stride=2), :] = pltpu.roll(pieces, SA, 1)
    out_ref[...] = os[...][:, :SA].astype(BF).reshape(out_ref.shape)


def final_group(dc, spot, pair, slab, turn, swap, u, got, out):
    near_spec = pl.BlockSpec((2, WIDE + 16, WIDE), lambda i, spot: (0, 0, 0))
    far_spec = pl.BlockSpec((1, WIDE + 16, WIDE), lambda i, spot: (0, 0, 0))
    more = [] if out is None else [out]
    return pl.pallas_call(
        final_kernel,
        grid_spec=pltpu.PrefetchScalarGridSpec(
            num_scalar_prefetch=1,
            grid=(2,),
            in_specs=[
                pl.BlockSpec((1, 1, WIDE, 1), lambda i, spot: (spot[1] ^ dc, i ^ spot[0], 0, 0)),
                pl.BlockSpec(slab.shape, lambda i, spot: (0, 0)),
                pl.BlockSpec(turn.shape, lambda i, spot: (0, 0)),
                pl.BlockSpec(swap.shape, lambda i, spot: (0, 0)),
                pl.BlockSpec((1, WIDE, 4 * WIDE), lambda i, spot: (i ^ spot[0], 0, 0)),
            ]
            + [near_spec, far_spec, far_spec, near_spec, near_spec]
            + [ANY] * len(more),
            out_specs=pl.BlockSpec(
                (16, 1, 16, 1, VBLK, SA), lambda i, spot: (0, spot[1] ^ dc, 0, i ^ spot[0], 0, 0)
            ),
            scratch_shapes=[
                pltpu.VMEM((4, WIDE + 16, WIDE), jnp.int16),
                pltpu.VMEM((4, WIDE, WIDE), F32),
                pltpu.VMEM((WIDE * VBLK, LANES), F32),
            ],
        ),
        out_shape=jax.ShapeDtypeStruct((16, 4, 16, 2, VBLK, SA), BF),
        input_output_aliases={11: 0} if more else {},
        compiler_params=PARAMS,
        cost_estimate=cost(2e9, 10e6),
    )(spot, pair, slab, turn, swap, u, *got, *more)


def partners(sizes, row, col, vir):
    n_row, n_col, n_vir = sizes
    found = []
    for r in range(n_row):
        for c in range(n_col):
            for z in range(n_vir):
                mine = (r * n_col + c) * n_vir + z
                other = ((r ^ row) * n_col + (c ^ col)) * n_vir + (z ^ vir)
                found.append((mine, other))
    return found


def packed_local(amplitudes, integrals, hole_integrals, irreps, occ_energy, vir_energy):
    vir_pos = lax.axis_index("vir")
    row_pos = lax.axis_index("row")
    col_pos = lax.axis_index("col")
    sizes = tuple(lax.axis_size(axis) for axis in AXES)
    n_row, n_col, n_vir = sizes
    occ_a, occ_h = amplitudes.shape[0], amplitudes.shape[2]
    groups = occ_a // n_col

    def swap_with(value, row, col, vir):
        if not (row or col or vir):
            return value
        return lax.ppermute(value, AXES, partners(sizes, row, col, vir))

    def place(first):
        return jnp.stack([row_pos, col_pos, vir_pos, first]).astype(jnp.int32)

    spot = place(0)
    high, low = np.arange(WIDE) // VBLK, np.arange(WIDE) % VBLK
    place_of, named = np.array(PLACE), np.array(NAMED)
    eye = np.eye(WIDE, dtype=np.float32)
    flip = jnp.asarray(eye[low * VBLK + high], BF)
    by_b = jnp.asarray(eye[place_of[low] * VBLK + high], BF)
    swap = jnp.asarray(eye[place_of[low] * VBLK + named[high]], BF)
    shard = jnp.transpose(integrals, (0, 2, 1, 3))

    def later(spot, *values):
        spot, *values = lax.optimization_barrier((spot, *values))
        return spot, *values

    def gather(mine, beside=lambda values: values, after=lambda values: values):
        over = lax.dynamic_index_in_dim(mine, (vir_pos ^ 3) % 2, 0, True)
        across, beyond = swap_with(mine, 0, 2, 0), swap_with(mine, 1, 0, 0)
        overs = [swap_with(over, 0, 0, 3), swap_with(over, 1, 0, 3)]
        across, *overs = beside([across, *overs])
        over = jnp.where(vir_pos // 2 == row_pos, *overs)
        near = [across, beyond, swap_with(across, 1, 0, 0), over, swap_with(over, 0, 2, 0)]
        near = jnp.concatenate([mine] + after(near), axis=0)
        return near, swap_with(near, 0, 1, 0)

    every = irreps.reshape(1, n_col, -1) == jnp.arange(8, dtype=irreps.dtype)[:, None, None]
    fullest = jnp.max(jnp.sum(every.astype(jnp.int32), axis=-1))

    energy_i = lax.dynamic_index_in_dim(occ_energy.reshape(groups, n_col, n_row), row_pos, 2, False)
    energy_j = lax.dynamic_index_in_dim(occ_energy.reshape(occ_h, n_col, n_row), col_pos, 1, False)
    pair = energy_i.T[:, None, None, :] + energy_j.T[None, :, :, None]
    pair = pair.reshape(n_col, n_row, occ_h * groups, 1)
    energies = vir_energy.reshape(n_vir, VBLK)
    energy_a = lax.dynamic_index_in_dim(energies, vir_pos, 0, False)[named]
    energy_b = jnp.take(energies, vir_pos ^ jnp.arange(n_vir), axis=0)
    slab_sum = (energy_a[None, :, None] + energy_b[:, None, :]).reshape(1, n_vir * WIDE)

    mine = pack(spot, irreps, by_b, shard)
    spot, mine = later(spot, mine)

    amps = jnp.transpose(amplitudes.reshape(groups, n_col, occ_h, n_row, CW, NV), (0, 1, 2, 4, 3, 5))
    first, slab = chunk_amplitudes(spot, amps, (3, 1))
    spot, first, slab = later(spot, first, slab)
    state = {"spot": spot, "slabs": [slab, swap_with(slab, 0, 2, 0)]}

    def hold(values):
        state["spot"], *values = later(state["spot"], *values)
        return values

    def hold_second(values):
        state["second"], slab = chunk_amplitudes(state["spot"], amps, (2, 0))
        state["spot"], state["second"], slab = later(state["spot"], state["second"], slab)
        *values, state["slabs"][1] = hold([*values, state["slabs"][1]])
        state["slabs"] += [slab, swap_with(slab, 0, 2, 0)]
        return values

    near, far = gather(mine, hold, hold_second)
    spot, slabs = state["spot"], state["slabs"]
    holes = jnp.transpose(hole_integrals.reshape(NO, occ_h, n_row, CW, SA), (2, 3, 4, 1, 0))
    spot, near, holes, pair, slab_sum, fullest = later(spot, near, holes, pair, slab_sum, fullest)
    rows_of = [(first, 0), (first, 1), (state["second"], 0), (state["second"], 1)]
    spot, far, slabs[3] = later(spot, far, slabs[3])
    slabs = jnp.stack(slabs)
    slabs_far = swap_with(slabs, 0, 1, 0)
    dense = unpack(spot, irreps, near, far, n_col)
    dense, slabs_far = lax.optimization_barrier((dense, slabs_far))

    k = np.arange(NO)
    order = np.zeros((n_col, CW, NO, LANES), np.float32)
    per_shard = NO // n_col
    for c in range(CW):
        lane = c * per_shard + (k // (n_row * n_col)) * n_row + k % n_row
        order[(k // n_row) % n_col, c, k, lane] = 1
    order = jnp.asarray(order.reshape(n_col, CW * NO, LANES), BF)

    def another(first):
        here = place(first)
        near, far = gather(pack(here, irreps, by_b, shard))
        return unpack(here, irreps, near, far, n_col)

    dense = lax.while_loop(
        lambda state: state[0] < fullest,
        lambda state: (state[0] + ROOM, state[1] + another(state[0])),
        (jnp.int32(ROOM), dense),
    )[1]

    def sum_group(chunk, spot, out):
        dc, u, got = chunk
        return final_group(dc, spot, pair, slab_sum, flip, swap, u, got, out)

    def arrive(chunk, spot, *waited):
        held = [chunk[2][name] for name in waited]
        spot, held = lax.optimization_barrier((spot, held))
        chunk[2].update(zip(waited, held))
        far = chunk[2]["far"]
        on = swap_with(jnp.stack([piece[1] for piece in far]), 1, 0, 0)
        chunk[2] = [chunk[2]["near"][0], *far, chunk[2]["near"][1], on]
        return spot

    out = None
    chunks = []
    for turn, dc in enumerate((3, 1, 2, 0)):
        if turn >= 2:
            spot = arrive(chunks[turn - 2], spot, "near", "far")
        if turn == 3:
            out = sum_group(chunks[0], spot, out)
            spot, out = lax.optimization_barrier((spot, out))
        u, near0, near1, one, two = mixed_group(
            dc, spot, *rows_of[turn], dense, holes, order, slabs, slabs_far, n_col
        )
        sent = {
            "near": [swap_with(near0, 0, dc, 0), swap_with(near1, 1, dc, 0)],
            "far": [swap_with(one, 0, dc, 1), swap_with(two, 0, dc, 2)],
        }
        spot, u = lax.optimization_barrier((spot, u))
        chunks.append([dc, u, sent])
    spot = arrive(chunks[2], spot, "near", "far")
    out = sum_group(chunks[1], spot, out)
    spot, out = lax.optimization_barrier((spot, out))
    spot = arrive(chunks[3], spot, "far")
    for turn in (2, 3):
        out = sum_group(chunks[turn], spot, out)
    return out.reshape(occ_a, 1, occ_h, 1, n_row, VBLK, SA)


def masked_block(piece, lab_a, lab_b, lab_c, lab_d):
    left = jnp.bitwise_xor(lab_a[:, None], lab_b[None, :])
    right = jnp.bitwise_xor(lab_c[:, None], lab_d[None, :])
    keep = left[:, :, None, None] == right[None, None, :, :]
    return jnp.where(keep, piece, jnp.zeros_like(piece))


def contract(amp_rows, block):
    return lax.dot_general(
        amp_rows, block, (((1, 2), (2, 3)), ((), ())), preferred_element_type=jnp.float32
    )


def plain_local(amplitudes, integrals, hole_integrals, irreps, occ_energy, vir_energy):
    vir_pos = lax.axis_index("vir")
    row_pos = lax.axis_index("row")
    col_pos = lax.axis_index("col")
    n_row = lax.axis_size("row")
    n_col = lax.axis_size("col")
    occ_a = amplitudes.shape[0]
    occ_h = amplitudes.shape[2]
    width_a = integrals.shape[0]
    pairs = occ_a * occ_h * n_row
    labels = jnp.repeat(irreps, VBLK)
    lab_a = lax.dynamic_slice_in_dim(labels, vir_pos * width_a, width_a)
    lab_c = labels[:CW]
    amp_rows = amplitudes.reshape(pairs, CW, NV)
    full_d = lax.all_gather(integrals, "col", axis=3, tiled=True)
    piece = lax.all_gather(full_d, "row", axis=1, tiled=True)
    lab_b = lax.slice_in_dim(labels, 0, piece.shape[1], axis=0)
    ladder = contract(amp_rows, masked_block(piece, lab_a, lab_b, lab_c, labels))
    slab_part = lax.dynamic_slice_in_dim(amplitudes, vir_pos * width_a, width_a, 6)
    every_k = lax.all_gather(slab_part, "col", axis=3, tiled=True).reshape(occ_a, NO, CW, width_a)
    hole_mat = hole_integrals.reshape(NO, occ_h * n_row, CW, SA)
    crossed = -lax.dot_general(
        every_k, hole_mat, (((1, 2), (0, 2)), ((), ())), preferred_element_type=jnp.float32
    )
    crossed = jnp.transpose(crossed, (0, 2, 1, 3)).reshape(pairs, width_a, SA)
    mixed = ladder + crossed
    groups = occ_a // n_col
    outgoing = mixed.reshape(groups, n_col, occ_h, n_row, width_a, SA)
    outgoing = jnp.transpose(outgoing, (3, 1, 0, 2, 4, 5)).reshape(
        n_row * n_col, groups, occ_h, width_a, SA
    )
    incoming = lax.all_to_all(
        lax.all_to_all(outgoing, ("row", "col"), split_axis=0, concat_axis=0, tiled=True),
        "vir",
        split_axis=4,
        concat_axis=3,
        tiled=True,
    )
    incoming = incoming.reshape(n_row, n_col, groups, occ_h, SA, width_a)
    mirrored = jnp.transpose(incoming, (3, 1, 2, 0, 5, 4)).reshape(pairs, width_a, SA)
    energy_i = lax.dynamic_slice_in_dim(occ_energy.reshape(occ_a, n_row), row_pos, 1, 1).reshape(
        occ_a
    )
    energy_j = lax.dynamic_slice_in_dim(
        occ_energy.reshape(occ_h, n_col, n_row), col_pos, 1, 1
    ).reshape(occ_h * n_row)
    energy_a = lax.dynamic_slice_in_dim(vir_energy, vir_pos * width_a, width_a)
    pair_sum = (energy_i[:, None] + energy_j[None, :]).reshape(pairs)
    denom = pair_sum[:, None, None] - energy_a[None, :, None] - vir_energy[None, None, :]
    result = ((mixed + mirrored) / denom).astype(jnp.bfloat16)
    return result.reshape(occ_a, 1, occ_h, 1, n_row, width_a, SA)


def solution(mesh):
    in_specs = (
        P(None, "row", None, "col", None, None, None),
        P("vir", "row", None, "col"),
        P(None, None, "col", None, None, None),
        P(),
        P(),
        P(),
    )
    out_specs = P(None, "row", None, "col", None, "vir", None)
    sizes = tuple(mesh.shape[axis] for axis in AXES)
    body = packed_local if sizes == (2, 4, 4) else plain_local
    return jax.shard_map(body, mesh=mesh, in_specs=in_specs, out_specs=out_specs, check_vma=False)
```

```python
import functools

import jax
import jax.numpy as jnp
import numpy as np
from jax import lax
from jax.experimental import pallas as pl
from jax.experimental.pallas import tpu as pltpu
from jax.sharding import PartitionSpec as P

NO = 128
NV = 1792
SA = 64
CW = 3
VBLK = 16

LANES = 128
WIDE = VBLK * VBLK
ROOM = 10
AXES = ("row", "col", "vir")
BF = jnp.bfloat16
F32 = jnp.float32
GRAIN = 64.0
TOP = 32000.0
PARAMS = pltpu.CompilerParams(vmem_limit_bytes=56 * 1024 * 1024)
ANY = pl.BlockSpec(memory_space=pl.ANY)
PLACE = [b // 8 * 8 + b % 2 * 4 + b % 8 // 2 for b in range(VBLK)]
NAMED = [PLACE.index(p) for p in range(VBLK)]


def nt(left, right):
    return lax.dot_general(left, right, (((1,), (1,)), ((), ())), preferred_element_type=F32)


def cost(flops, moved):
    return pl.CostEstimate(flops=int(flops), bytes_accessed=int(moved), transcendentals=0)


def pack_kernel(spot_ref, irr_ref, turn_ref, v_ref, out_ref):
    depth = v_ref.shape[3]
    count = depth // VBLK
    lane = lax.broadcasted_iota(jnp.int32, (1, depth), 1)
    row = lax.broadcasted_iota(jnp.int32, (ROOM * VBLK, depth), 0)
    for half in range(2):
        label = irr_ref[spot_ref[2]] ^ irr_ref[2 * spot_ref[0] + half] ^ irr_ref[0]
        held = -spot_ref[3]
        target = jnp.full((1, depth), -1, jnp.int32)
        for block in range(count):
            match = irr_ref[spot_ref[1] * count + block] == label
            start = jnp.where(match & (held >= 0), held * VBLK, -NV)
            target = jnp.where(lane // VBLK == block, start + lane % VBLK, target)
            held = held + match.astype(jnp.int32)
        pick = (row == target).astype(F32).astype(BF)
        for c in range(CW):
            part = v_ref[:, c, half * VBLK : (half + 1) * VBLK, :].reshape(WIDE, depth)
            packed = nt(pick, part).astype(BF)
            out_ref[half, c] = jnp.dot(packed, turn_ref[...], preferred_element_type=F32).astype(BF)


def pack(spot, irreps, turn, v):
    return pl.pallas_call(
        pack_kernel,
        grid_spec=pltpu.PrefetchScalarGridSpec(
            num_scalar_prefetch=2,
            grid=(1,),
            in_specs=[
                pl.BlockSpec(turn.shape, lambda i, *_: (0, 0)),
                pl.BlockSpec(v.shape, lambda i, *_: (0, 0, 0, 0)),
            ],
            out_specs=pl.BlockSpec((2, CW, ROOM * VBLK, WIDE), lambda i, *_: (0, 0, 0, 0)),
        ),
        out_shape=jax.ShapeDtypeStruct((2, CW, ROOM * VBLK, WIDE), BF),
        compiler_params=PARAMS,
        cost_estimate=cost(4e8, 2e6),
    )(spot, irreps, turn, v)


def unpack_kernel(n_col, spot_ref, irr_ref, near_ref, far_ref, out_ref, found_ref):
    step = pl.program_id(0)
    other = spot_ref[2] ^ jnp.where(step == 0, 3, step - 1)
    label = irr_ref[spot_ref[2]] ^ irr_ref[other] ^ irr_ref[0]
    away = ((other // 2) != spot_ref[0]).astype(jnp.int32)
    base = jnp.where(step == 0, 8, away * 4 + other % 2)
    pace = jnp.where(step == 0, 1, 2)
    depth = NV // n_col
    count = depth // VBLK
    out_ref[...] = jnp.zeros(out_ref.shape, BF)
    for dc in range(n_col):
        shard = spot_ref[1] ^ dc
        piece_ref = far_ref if dc % 2 else near_ref
        which = base + (dc // 2) * pace

        def note(block, held):
            found_ref[jnp.clip(held + 1, 0, ROOM + 1)] = block
            return held + (irr_ref[shard * count + block] == label).astype(jnp.int32)

        held = lax.fori_loop(0, count, note, -spot_ref[3], unroll=count)

        def move(place, _):
            row = shard * depth + found_ref[place + 1] * VBLK
            for c in range(CW):
                out_ref[pl.ds(pl.multiple_of(c * NV + row, VBLK), VBLK), :] = piece_ref[
                    which, c, pl.ds(pl.multiple_of(place * VBLK, VBLK), VBLK), :
                ]
            return 0

        lax.fori_loop(0, jnp.clip(held, 0, ROOM), move, 0)


def unpack(spot, irreps, near, far, n_col):
    whole = pl.BlockSpec(near.shape, lambda t, *_: (0, 0, 0, 0))
    return pl.pallas_call(
        functools.partial(unpack_kernel, n_col),
        grid_spec=pltpu.PrefetchScalarGridSpec(
            num_scalar_prefetch=2,
            grid=(5,),
            in_specs=[whole, whole],
            out_specs=pl.BlockSpec((CW * NV, WIDE), lambda t, *_: (0, t)),
            scratch_shapes=[pltpu.SMEM((ROOM + 2,), jnp.int32)],
        ),
        out_shape=jax.ShapeDtypeStruct((CW * NV, 5 * WIDE), BF),
        compiler_params=PARAMS,
        cost_estimate=cost(1e6, 18e6),
    )(spot, irreps, near, far)


def chunk_kernel(spot_ref, t_ref, out_ref, slab_ref):
    groups, occ_h = t_ref.shape[0], t_ref.shape[2]
    rows = 2 * occ_h
    first = []
    for c in range(CW):
        part = t_ref[:, 0, :, c, :, :].reshape(groups * rows, NV)
        out_ref[0, :, c * NV : (c + 1) * NV] = part
        first.append(part[:, :LANES])
    row = lax.broadcasted_iota(jnp.int32, (2 * VBLK, LANES), 0)
    lane = lax.broadcasted_iota(jnp.int32, (2 * VBLK, LANES), 1)
    block = jnp.where(row < VBLK, spot_ref[2], spot_ref[2] ^ 3)
    pick = (lane == block * VBLK + row % VBLK).astype(F32).astype(BF)
    empty = jnp.zeros((rows, LANES), BF)
    for q in range(groups):
        some = jnp.concatenate([x[q * rows : (q + 1) * rows] for x in first] + [empty], axis=0)
        found = nt(pick, some).astype(BF)
        for far in range(2):
            slab_ref[far, 0, q * VBLK : (q + 1) * VBLK, :] = found[far * VBLK : (far + 1) * VBLK]


def chunk_amplitudes(spot, t, dcs):
    q4, n_col, occ_h, _, n_row, _ = t.shape
    some = 4
    rows = occ_h * n_row

    def group(i, spot):
        return spot[1] ^ jnp.where(i == 0, dcs[0], dcs[-1])

    return pl.pallas_call(
        chunk_kernel,
        grid_spec=pltpu.PrefetchScalarGridSpec(
            num_scalar_prefetch=1,
            grid=(len(dcs), q4 // some),
            in_specs=[
                pl.BlockSpec(
                    (some, 1, occ_h, CW, n_row, NV), lambda i, q, spot: (q, group(i, spot), 0, 0, 0, 0)
                )
            ],
            out_specs=[
                pl.BlockSpec((1, some * rows, CW * NV), lambda i, q, _: (i, q, 0)),
                pl.BlockSpec((2, 1, some * VBLK, LANES), lambda i, q, _: (0, i, q, 0)),
            ],
        ),
        out_shape=[
            jax.ShapeDtypeStruct((len(dcs), q4 * rows, CW * NV), BF),
            jax.ShapeDtypeStruct((2, len(dcs), q4 * VBLK, LANES), BF),
        ],
        compiler_params=PARAMS,
        cost_estimate=cost(1e8, 23e6),
    )(spot, t)


def trade_lanes(x, bits):
    piece = lax.broadcasted_iota(jnp.int32, x[0].shape, 1) // VBLK
    for k in range(bits):
        bit = 1 << k
        upper = (piece & bit) != 0
        y = []
        for i in range(1 << bits):
            if i & bit:
                moved = pltpu.roll(x[i ^ bit], LANES - bit * VBLK, 1)
                y.append(jnp.where(upper, x[i], moved))
            else:
                moved = pltpu.roll(x[i ^ bit], bit * VBLK, 1)
                y.append(jnp.where(upper, moved, x[i]))
        x = y
    return x


def mixed_kernel(n_col, spot_ref, t_ref, v_ref, w_ref, order_ref, *refs):
    parts, refs = refs[:n_col], refs[n_col:]
    u_ref, near_ref, one_ref, two_ref, acc, zs, ints, slabs = refs
    step = pl.program_id(0)
    rows = 2 * WIDE

    def product():
        return jnp.dot(t_ref[0], v_ref[...], preferred_element_type=F32)

    def keep(ladder):
        for half in range(2):
            acc[half] = ladder[:, half * LANES : (half + 1) * LANES]

    def rest():
        holes = jnp.concatenate([w_ref[:, c].reshape(rows, NO) for c in range(CW)], axis=1)
        slab = slabs[(step == 1).astype(jnp.int32)]
        cross = jnp.dot(holes, slab, preferred_element_type=F32)
        for half in range(2):
            zs[half] = cross[:, half * LANES : (half + 1) * LANES]
        for lt in range(2):
            for s in range(2):
                for half in range(2):
                    for hh in range(2):
                        first = [
                            s * WIDE + NAMED[half * 8 + i] * VBLK + hh * 8 for i in range(8)
                        ]
                        x = trade_lanes([zs[lt, at : at + 8, :] for at in first], 3)
                        for j in range(8):
                            q4 = lt * 8 + j
                            have = acc[half, pl.ds(q4 * 32 + hh * 16 + s, 8, stride=2), :]
                            u_ref[
                                s, q4 * 16 + hh * 8 : q4 * 16 + hh * 8 + 8,
                                half * LANES : (half + 1) * LANES,
                            ] = have - x[j]
        for dr in range(2):
            value = u_ref[spot_ref[0] ^ dr]
            most = jnp.maximum(jnp.max(jnp.abs(value), axis=0, keepdims=True), 1e-30)
            grade = jnp.ceil(jnp.log2(most) * GRAIN)
            scale = TOP * jnp.exp2(-grade / GRAIN)
            whole = ((value * scale + 32768.5).astype(jnp.int32) - 32768).astype(jnp.int16)
            grades = jnp.broadcast_to(grade, (16, WIDE)).astype(jnp.int32).astype(jnp.int16)
            ints[dr, :WIDE, :] = whole
            ints[dr, WIDE:, :] = grades

    @pl.when(step == 0)
    def _():
        order = jnp.concatenate([order_ref[spot_ref[1] ^ dc] for dc in range(n_col)], axis=1)
        for far in range(2):
            pieces = jnp.concatenate([part[0, far, 0] for part in parts], axis=1)
            slabs[far] = nt(order, pieces).astype(BF)
        keep(product())

    @pl.when((step > 0) & (step < 5))
    def _():
        ladder = product()
        rest()
        keep(ladder)

    @pl.when(step == 5)
    def _():
        rest()

    def send(outs):
        for dr in range(2):
            outs[dr][...] = ints[dr]

    for n, outs in (
        (1, (near_ref.at[0, 1], near_ref.at[1, 1])),
        (2, (near_ref.at[0, 0], near_ref.at[1, 0])),
        (3, (one_ref.at[0], one_ref.at[1])),
        (4, (two_ref.at[0], two_ref.at[1])),
    ):
        pl.when(step == n)(functools.partial(send, outs))


def mixed_group(dc, spot, t, at, v, w, order, slabs, slabs_far, n_col):
    ints = jax.ShapeDtypeStruct((2, WIDE + 16, WIDE), jnp.int16)
    ints_spec = pl.BlockSpec(ints.shape, lambda n, spot: (0, 0, 0))
    near = jax.ShapeDtypeStruct((2,) + ints.shape, jnp.int16)
    near_spec = pl.BlockSpec(near.shape, lambda n, spot: (0, 0, 0, 0))

    def slab_spec(other):
        group = dc ^ other
        which = (2 if group % 2 == 0 else 0) + other // 2
        return pl.BlockSpec(
            (1, 2, 1, WIDE, LANES), lambda n, spot: (which, 0, int(group < 2), 0, 0)
        )

    return pl.pallas_call(
        functools.partial(mixed_kernel, n_col),
        grid_spec=pltpu.PrefetchScalarGridSpec(
            num_scalar_prefetch=1,
            grid=(6,),
            in_specs=[
                pl.BlockSpec((1,) + t.shape[1:], lambda n, spot: (at, 0, 0)),
                pl.BlockSpec((CW * NV, WIDE), lambda n, spot: (0, jnp.minimum(n, 4))),
                pl.BlockSpec(
                    (2, CW, VBLK, w.shape[3], NO),
                    lambda n, spot: (0, 0, spot[2] ^ jnp.maximum(n - 2, 0), 0, 0),
                ),
                pl.BlockSpec(order.shape, lambda n, spot: (0, 0, 0)),
            ]
            + [slab_spec(other) for other in range(n_col)],
            out_specs=[
                pl.BlockSpec((2, WIDE, WIDE), lambda n, spot: (0, 0, jnp.clip(n - 2, 0, 3)))
            ]
            + [near_spec, ints_spec, ints_spec],
            scratch_shapes=[
                pltpu.VMEM((2, 2 * WIDE, LANES), F32),
                pltpu.VMEM((2, 2 * WIDE, LANES), F32),
                pltpu.VMEM((2, WIDE + 16, WIDE), jnp.int16),
                pltpu.VMEM((2, CW * NO, WIDE), BF),
            ],
        ),
        out_shape=[jax.ShapeDtypeStruct((2, WIDE, 4 * WIDE), F32), near, ints, ints],
        compiler_params=PARAMS,
        cost_estimate=cost(7.2e9, 24e6),
    )(spot, t, v, w, order, *([slabs, slabs_far] * 2))


def trade_rows(x):
    row = lax.broadcasted_iota(jnp.int32, x[0].shape, 0)
    for k in range(3):
        bit = 1 << k
        upper = (row & bit) != 0
        y = []
        for i in range(8):
            if i & bit:
                y.append(jnp.where(upper, x[i], pltpu.roll(x[i ^ bit], 8 - bit, 0)))
            else:
                y.append(jnp.where(upper, pltpu.roll(x[i ^ bit], bit, 0), x[i]))
        x = y
    return x


def final_kernel(split, dc, n_col, spot_ref, occ_ref, vir_ref, turn_ref, swap_ref, u_ref, *refs):
    got, (out_ref, ints, incs, os) = refs[:-4], refs[-4:]
    step = pl.program_id(0)
    for dr in range(2):

        @pl.when(step == dr)
        def _(dr=dr):
            if dr == 0:
                parts = [got[0].at[0, 0], got[1].at[0], got[2].at[0], got[0].at[0, 1]]
            elif split:
                parts = [got[3].at[0], got[4].at[0], got[4].at[1], got[3].at[1]]
            else:
                parts = [got[3].at[0], got[3].at[2], got[3].at[3], got[3].at[1]]
            for t, part in enumerate(parts):
                ints[t] = part[...]

    own = u_ref[0]
    high = own.astype(BF)
    low = (own - high.astype(F32)).astype(BF)
    both = jnp.concatenate([high, low], axis=1)
    both = jnp.dot(turn_ref[...], both, preferred_element_type=F32).astype(BF)
    both = jnp.concatenate([both[:, i * WIDE : (i + 1) * WIDE] for i in range(8)], axis=0)
    both = jnp.dot(both, swap_ref[...], preferred_element_type=F32)
    m, s = spot_ref[1] ^ dc, spot_ref[0] ^ step
    row = lax.broadcasted_iota(jnp.int32, (8, LANES), 0)
    first = []
    for q_half in range(2):
        energy = jnp.zeros((8, LANES), F32)
        for k in range(8):
            energy = jnp.where(row == k, occ_ref[((q_half * 8 + k) * n_col + m) * 2 + spot_ref[0]], energy)
        first.append(energy)
    pair = jnp.concatenate(
        [first[g % 2] + occ_ref[((g // 2) * n_col + spot_ref[1]) * 2 + s] for g in range(32)], axis=0
    )
    pair = jnp.concatenate([pair, pair], axis=1)
    lane = lax.broadcasted_iota(jnp.int32, (1, WIDE), 1)
    energy_a = jnp.zeros((1, WIDE), F32)
    for p in range(VBLK):
        energy_a = jnp.where(lane // VBLK == p, vir_ref[spot_ref[2] * VBLK + NAMED[p]], energy_a)
    for t in range(4):
        energy_b = jnp.zeros((1, WIDE), F32)
        for b in range(VBLK):
            energy_b = jnp.where(lane % VBLK == b, vir_ref[(spot_ref[2] ^ t) * VBLK + b], energy_b)
        mine = both[t * WIDE : (t + 1) * WIDE] + both[(t + 4) * WIDE : (t + 5) * WIDE]
        grade = ints[t, WIDE : WIDE + 16, :].astype(jnp.int32).astype(F32)[:1]
        scale = jnp.exp2(grade / GRAIN) / TOP
        mirror = ints[t, :WIDE, :].astype(jnp.int32).astype(F32) * scale
        incs[t] = (mine + mirror) / (pair - energy_a - energy_b)
    for h in range(16):
        for q_half in range(2):
            rows = slice(h * 16 + q_half * 8, h * 16 + q_half * 8 + 8)
            x = []
            for half in range(2):
                lanes = slice(half * LANES, (half + 1) * LANES)
                x += trade_lanes([incs[spot_ref[2] ^ b, rows, lanes] for b in range(4)], 2)
            for p, pieces in enumerate(trade_rows(x)):
                first = ((q_half * 8 + p) * 16 + h) * VBLK
                os[pl.ds(first, 8, stride=2), :] = pieces
                os[pl.ds(first + 1, 8, stride=2), :] = pltpu.roll(pieces, SA, 1)
    out_ref[...] = os[...][:, :SA].astype(BF).reshape(out_ref.shape)


def final_group(dc, n_col, spot, occ, vir, turn, swap, u, got, out):
    split = len(got) == 5
    got_specs = [pl.BlockSpec((1, 2, WIDE + 16, WIDE), lambda i, spot, *_: (0, 0, 0, 0))]
    got_specs += [pl.BlockSpec((1, WIDE + 16, WIDE), lambda i, spot, *_: (0, 0, 0))] * 2
    got_specs += [pl.BlockSpec(x.shape, lambda i, spot, *_: (0, 0, 0)) for x in got[3:]]
    more = [] if out is None else [out]
    return pl.pallas_call(
        functools.partial(final_kernel, split, dc, n_col),
        grid_spec=pltpu.PrefetchScalarGridSpec(
            num_scalar_prefetch=3,
            grid=(2,),
            in_specs=[
                pl.BlockSpec(turn.shape, lambda i, spot, *_: (0, 0)),
                pl.BlockSpec(swap.shape, lambda i, spot, *_: (0, 0)),
                pl.BlockSpec((1, WIDE, 4 * WIDE), lambda i, spot, *_: (i ^ spot[0], 0, 0)),
            ]
            + got_specs
            + [ANY] * len(more),
            out_specs=pl.BlockSpec(
                (16, 1, 16, 1, VBLK, SA), lambda i, spot, *_: (0, spot[1] ^ dc, 0, i ^ spot[0], 0, 0)
            ),
            scratch_shapes=[
                pltpu.VMEM((4, WIDE + 16, WIDE), jnp.int16),
                pltpu.VMEM((4, WIDE, WIDE), F32),
                pltpu.VMEM((WIDE * VBLK, LANES), F32),
            ],
        ),
        out_shape=jax.ShapeDtypeStruct((16, 4, 16, 2, VBLK, SA), BF),
        input_output_aliases={6 + len(got): 0} if more else {},
        compiler_params=PARAMS,
        cost_estimate=cost(2e9, 10e6),
    )(spot, occ, vir, turn, swap, u, *got, *more)


def partners(sizes, row, col, vir):
    n_row, n_col, n_vir = sizes
    found = []
    for r in range(n_row):
        for c in range(n_col):
            for z in range(n_vir):
                mine = (r * n_col + c) * n_vir + z
                other = ((r ^ row) * n_col + (c ^ col)) * n_vir + (z ^ vir)
                found.append((mine, other))
    return found


def packed_local(amplitudes, integrals, hole_integrals, irreps, occ_energy, vir_energy):
    vir_pos = lax.axis_index("vir")
    row_pos = lax.axis_index("row")
    col_pos = lax.axis_index("col")
    sizes = tuple(lax.axis_size(axis) for axis in AXES)
    n_row, n_col, n_vir = sizes
    occ_a, occ_h = amplitudes.shape[0], amplitudes.shape[2]
    groups = occ_a // n_col

    def swap_with(value, row, col, vir):
        if not (row or col or vir):
            return value
        return lax.ppermute(value, AXES, partners(sizes, row, col, vir))

    def place(first):
        return jnp.stack([row_pos, col_pos, vir_pos, first]).astype(jnp.int32)

    spot = place(0)
    high, low = np.arange(WIDE) // VBLK, np.arange(WIDE) % VBLK
    place_of, named = np.array(PLACE), np.array(NAMED)
    eye = np.eye(WIDE, dtype=np.float32)
    flip = jnp.asarray(eye[low * VBLK + high], BF)
    by_b = jnp.asarray(eye[place_of[low] * VBLK + high], BF)
    swap = jnp.asarray(eye[place_of[low] * VBLK + named[high]], BF)
    shard = jnp.transpose(integrals, (0, 2, 1, 3))

    def later(spot, *values):
        spot, *values = lax.optimization_barrier((spot, *values))
        return spot, *values

    def gather(mine, beside=lambda values: values, after=lambda values: values):
        over = lax.dynamic_index_in_dim(mine, (vir_pos ^ 3) % 2, 0, True)
        across, beyond = swap_with(mine, 0, 2, 0), swap_with(mine, 1, 0, 0)
        overs = [swap_with(over, 0, 0, 3), swap_with(over, 1, 0, 3)]
        across, *overs = beside([across, *overs])
        over = jnp.where(vir_pos // 2 == row_pos, *overs)
        near = [across, beyond, swap_with(across, 1, 0, 0), over, swap_with(over, 0, 2, 0)]
        near = jnp.concatenate([mine] + after(near), axis=0)
        return near, swap_with(near, 0, 1, 0)

    every = irreps.reshape(1, n_col, -1) == jnp.arange(8, dtype=irreps.dtype)[:, None, None]
    fullest = jnp.max(jnp.sum(every.astype(jnp.int32), axis=-1))

    mine = pack(spot, irreps, by_b, shard)
    spot, mine = later(spot, mine)

    amps = jnp.transpose(amplitudes.reshape(groups, n_col, occ_h, n_row, CW, NV), (0, 1, 2, 4, 3, 5))
    first, slab = chunk_amplitudes(spot, amps, (3, 1))
    spot, first, slab = later(spot, first, slab)
    state = {"spot": spot, "slabs": [slab, swap_with(slab, 0, 2, 0)]}

    def hold(values):
        state["spot"], *values = later(state["spot"], *values)
        return values

    def hold_second(values):
        state["second"], slab = chunk_amplitudes(state["spot"], amps, (2, 0))
        state["spot"], state["second"], slab = later(state["spot"], state["second"], slab)
        *values, state["slabs"][1] = hold([*values, state["slabs"][1]])
        state["slabs"] += [slab, swap_with(slab, 0, 2, 0)]
        return values

    near, far = gather(mine, hold, hold_second)
    spot, slabs = state["spot"], state["slabs"]
    holes = jnp.transpose(hole_integrals.reshape(NO, occ_h, n_row, CW, SA), (2, 3, 4, 1, 0))
    spot, near, holes, fullest = later(spot, near, holes, fullest)
    rows_of = [(first, 0), (first, 1), (state["second"], 0), (state["second"], 1)]
    spot, far, slabs[3] = later(spot, far, slabs[3])
    slabs = jnp.stack(slabs)
    slabs_far = swap_with(slabs, 0, 1, 0)
    dense = unpack(spot, irreps, near, far, n_col)
    dense, slabs_far = lax.optimization_barrier((dense, slabs_far))

    k = np.arange(NO)
    order = np.zeros((n_col, CW, NO, LANES), np.float32)
    per_shard = NO // n_col
    for c in range(CW):
        lane = c * per_shard + (k // (n_row * n_col)) * n_row + k % n_row
        order[(k // n_row) % n_col, c, k, lane] = 1
    order = jnp.asarray(order.reshape(n_col, CW * NO, LANES), BF)

    def another(first):
        here = place(first)
        near, far = gather(pack(here, irreps, by_b, shard))
        return unpack(here, irreps, near, far, n_col)

    dense = lax.while_loop(
        lambda state: state[0] < fullest,
        lambda state: (state[0] + ROOM, state[1] + another(state[0])),
        (jnp.int32(ROOM), dense),
    )[1]

    def sum_group(chunk, spot, out):
        dc, u, got = chunk
        return final_group(dc, n_col, spot, occ_energy, vir_energy, flip, swap, u, got, out)

    def arrive(chunk, spot, *waited):
        held = [chunk[2][name] for name in waited]
        spot, held = lax.optimization_barrier((spot, held))
        chunk[2].update(zip(waited, held))
        near, one, two = chunk[2]["near"], chunk[2]["one"], chunk[2]["two"]
        if "beyond" in chunk[2]:
            rest = [chunk[2]["beyond"], swap_with(jnp.stack([one[1], two[1]]), 1, 0, 0)]
        else:
            rest = [swap_with(jnp.concatenate([near[1], one[1:], two[1:]], axis=0), 1, 0, 0)]
        chunk[2] = [near, one, two, *rest]
        return spot

    out = None
    chunks = []
    for turn, dc in enumerate((3, 1, 2, 0)):
        if turn >= 2:
            spot = arrive(chunks[turn - 2], spot, "near", "one", "two")
        if turn == 3:
            out = sum_group(chunks[0], spot, out)
            spot, out = lax.optimization_barrier((spot, out))
        u, near, one, two = mixed_group(
            dc, spot, *rows_of[turn], dense, holes, order, slabs, slabs_far, n_col
        )
        sent = {
            "near": swap_with(near, 0, dc, 0),
            "one": swap_with(one, 0, dc, 1),
            "two": swap_with(two, 0, dc, 2),
        }
        if dc == 0:
            sent["beyond"] = swap_with(near[1], 1, 0, 0)
        spot, u = lax.optimization_barrier((spot, u))
        chunks.append([dc, u, sent])
    spot = arrive(chunks[2], spot, "near", "one", "two")
    out = sum_group(chunks[1], spot, out)
    spot, out = lax.optimization_barrier((spot, out))
    spot = arrive(chunks[3], spot, "one", "two")
    for turn in (2, 3):
        out = sum_group(chunks[turn], spot, out)
    return out.reshape(occ_a, 1, occ_h, 1, n_row, VBLK, SA)


def masked_block(piece, lab_a, lab_b, lab_c, lab_d):
    left = jnp.bitwise_xor(lab_a[:, None], lab_b[None, :])
    right = jnp.bitwise_xor(lab_c[:, None], lab_d[None, :])
    keep = left[:, :, None, None] == right[None, None, :, :]
    return jnp.where(keep, piece, jnp.zeros_like(piece))


def contract(amp_rows, block):
    return lax.dot_general(
        amp_rows, block, (((1, 2), (2, 3)), ((), ())), preferred_element_type=jnp.float32
    )


def plain_local(amplitudes, integrals, hole_integrals, irreps, occ_energy, vir_energy):
    vir_pos = lax.axis_index("vir")
    row_pos = lax.axis_index("row")
    col_pos = lax.axis_index("col")
    n_row = lax.axis_size("row")
    n_col = lax.axis_size("col")
    occ_a = amplitudes.shape[0]
    occ_h = amplitudes.shape[2]
    width_a = integrals.shape[0]
    pairs = occ_a * occ_h * n_row
    labels = jnp.repeat(irreps, VBLK)
    lab_a = lax.dynamic_slice_in_dim(labels, vir_pos * width_a, width_a)
    lab_c = labels[:CW]
    amp_rows = amplitudes.reshape(pairs, CW, NV)
    full_d = lax.all_gather(integrals, "col", axis=3, tiled=True)
    piece = lax.all_gather(full_d, "row", axis=1, tiled=True)
    lab_b = lax.slice_in_dim(labels, 0, piece.shape[1], axis=0)
    ladder = contract(amp_rows, masked_block(piece, lab_a, lab_b, lab_c, labels))
    slab_part = lax.dynamic_slice_in_dim(amplitudes, vir_pos * width_a, width_a, 6)
    every_k = lax.all_gather(slab_part, "col", axis=3, tiled=True).reshape(occ_a, NO, CW, width_a)
    hole_mat = hole_integrals.reshape(NO, occ_h * n_row, CW, SA)
    crossed = -lax.dot_general(
        every_k, hole_mat, (((1, 2), (0, 2)), ((), ())), preferred_element_type=jnp.float32
    )
    crossed = jnp.transpose(crossed, (0, 2, 1, 3)).reshape(pairs, width_a, SA)
    mixed = ladder + crossed
    groups = occ_a // n_col
    outgoing = mixed.reshape(groups, n_col, occ_h, n_row, width_a, SA)
    outgoing = jnp.transpose(outgoing, (3, 1, 0, 2, 4, 5)).reshape(
        n_row * n_col, groups, occ_h, width_a, SA
    )
    incoming = lax.all_to_all(
        lax.all_to_all(outgoing, ("row", "col"), split_axis=0, concat_axis=0, tiled=True),
        "vir",
        split_axis=4,
        concat_axis=3,
        tiled=True,
    )
    incoming = incoming.reshape(n_row, n_col, groups, occ_h, SA, width_a)
    mirrored = jnp.transpose(incoming, (3, 1, 2, 0, 5, 4)).reshape(pairs, width_a, SA)
    energy_i = lax.dynamic_slice_in_dim(occ_energy.reshape(occ_a, n_row), row_pos, 1, 1).reshape(
        occ_a
    )
    energy_j = lax.dynamic_slice_in_dim(
        occ_energy.reshape(occ_h, n_col, n_row), col_pos, 1, 1
    ).reshape(occ_h * n_row)
    energy_a = lax.dynamic_slice_in_dim(vir_energy, vir_pos * width_a, width_a)
    pair_sum = (energy_i[:, None] + energy_j[None, :]).reshape(pairs)
    denom = pair_sum[:, None, None] - energy_a[None, :, None] - vir_energy[None, None, :]
    result = ((mixed + mirrored) / denom).astype(jnp.bfloat16)
    return result.reshape(occ_a, 1, occ_h, 1, n_row, width_a, SA)


def solution(mesh):
    in_specs = (
        P(None, "row", None, "col", None, None, None),
        P("vir", "row", None, "col"),
        P(None, None, "col", None, None, None),
        P(),
        P(),
        P(),
    )
    out_specs = P(None, "row", None, "col", None, "vir", None)
    sizes = tuple(mesh.shape[axis] for axis in AXES)
    body = packed_local if sizes == (2, 4, 4) else plain_local
    return jax.shard_map(body, mesh=mesh, in_specs=in_specs, out_specs=out_specs, check_vma=False)
```
